32 devices in a mesh: dp: 4 (over y, x), fsdp: 8 (over z, core).
Axes of the slice: x: 2, y: 2, z: 4, core: 2. Of those that a mesh axis runs over, the one named last changes fastest.
Arguments:
- inputs: bfloat16 [8, 512, 2048], P('dp', 'fsdp'), may hold values from -11.2 to 11.2
- block_ids: int32 [8, 512], P('dp'), may hold values from 0 to 3, never falling along the last dimension, each value on 1 to 256 neighbouring positions
- cotangent: bfloat16 [8, 512, 2048], P('dp', 'fsdp'), may hold values from -6 to 6
- ln1_gain: bfloat16 [2048], P(('dp', 'fsdp')), may hold values from 0.25 to 1.75
- ln1_bias: bfloat16 [2048], P(('dp', 'fsdp')), may hold values from -1.5 to 1.5
- query_weight: bfloat16 [2048, 2048], P(('dp', 'fsdp')), may hold values from -0.25 to 0.25
- query_bias: bfloat16 [2048], P(('dp', 'fsdp')), may hold values from -1.5 to 1.5
- key_weight: bfloat16 [2048, 2048], P(('dp', 'fsdp')), may hold values from -0.125 to 0.125
- value_weight: bfloat16 [2048, 2048], P(('dp', 'fsdp')), may hold values from -0.125 to 0.125
- value_bias: bfloat16 [2048], P(('dp', 'fsdp')), may hold values from -1.5 to 1.5
- out_weight: bfloat16 [2048, 2048], P(('dp', 'fsdp')), may hold values from -0.5 to 0.5
- out_bias: bfloat16 [2048], P(('dp', 'fsdp')), may hold values from -1.5 to 1.5
- ln2_gain: bfloat16 [2048], P(('dp', 'fsdp')), may hold values from 0.25 to 1.75
- ln2_bias: bfloat16 [2048], P(('dp', 'fsdp')), may hold values from -1.5 to 1.5
- up_weight: bfloat16 [2048, 8192], P(('dp', 'fsdp')), may hold values from -0.125 to 0.125
- up_bias: bfloat16 [8192], P(('dp', 'fsdp')), may hold values from -1.5 to 1.5
- down_weight: bfloat16 [8192, 2048], P(('dp', 'fsdp')), may hold values from -0.09375 to 0.09375
- down_bias: bfloat16 [2048], P(('dp', 'fsdp')), may hold values from -1.5 to 1.5
Outputs:
- output: bfloat16 [8, 512, 2048], P('dp', 'fsdp')
- input_grad: float32 [8, 512, 2048], P('dp', 'fsdp')
- ln1_gain_grad: float32 [2048], P(('dp', 'fsdp'))
- ln1_bias_grad: float32 [2048], P(('dp', 'fsdp'))
- query_weight_grad: float32 [2048, 2048], P(('dp', 'fsdp'))
- query_bias_grad: float32 [2048], P(('dp', 'fsdp'))
- key_weight_grad: float32 [2048, 2048], P(('dp', 'fsdp'))
- value_weight_grad: float32 [2048, 2048], P(('dp', 'fsdp'))
- value_bias_grad: float32 [2048], P(('dp', 'fsdp'))
- out_weight_grad: float32 [2048, 2048], P(('dp', 'fsdp'))
- out_bias_grad: float32 [2048], P(('dp', 'fsdp'))
- ln2_gain_grad: float32 [2048], P(('dp', 'fsdp'))
- ln2_bias_grad: float32 [2048], P(('dp', 'fsdp'))
- up_weight_grad: float32 [2048, 8192], P(('dp', 'fsdp'))
- up_bias_grad: float32 [8192], P(('dp', 'fsdp'))
- down_weight_grad: float32 [8192, 2048], P(('dp', 'fsdp'))
- down_bias_grad: float32 [2048], P(('dp', 'fsdp'))
- rms_input: float32 [], replicated
- rms_attention: float32 [], replicated
- rms_mlp: float32 [], replicated
The draws below stay inside these ranges and needn't reach their ends.
Inputs may be any that keep to these rules, and one draw needn't show every extreme that they name: `block_ids`: block ids never fall along a sequence; positions with one id form one attention block of 1 to 256 positions.
All inputs are finite; a program needn't handle non-finite values.
Results may differ from the reference program's by a relative error of at most 0.018.
Values may be sent and summed in bfloat16 or wider, within the bound.
No kernel may reach another device: no remote copies, remote signals or barrier semaphores. Data moves between devices by JAX's collectives and lax.ppermute only.
A program may use at most 448 MiB of HBM per device.

```python
import math
import jax
import jax.numpy as jnp
import numpy as np
from jax import lax

D = 2048
HEADS = 16
HEAD = 128
FF = 8192
BLOCK = 256
SEQS = 8
LENGTH = 512


def draw_inputs(key, part):
    noise_key = jax.random.fold_in(key, 0)
    seq_scale = 0.6 + 1.2 * jnp.arange(SEQS, dtype=jnp.float32) / max(SEQS - 1, 1)
    pos_scale = 0.6 + 1.2 * jnp.arange(LENGTH, dtype=jnp.float32) / max(LENGTH - 1, 1)
    scales = seq_scale[:, None, None] * pos_scale[None, :, None]
    base = jnp.clip(jax.random.normal(noise_key, (SEQS, LENGTH, D), jnp.float32), -3.0, 3.0)
    return (base * scales).astype(jnp.bfloat16)


def shard_levels(key, shape, cuts, smallest, high):
    loudness = 1.0
    for axis_at, parts in cuts:
        heights = jax.random.uniform(jax.random.fold_in(jax.random.fold_in(key, 6), axis_at), (parts,), jnp.float32, smallest / len(cuts), high / len(cuts))
        loudness = loudness * jnp.repeat(jnp.exp(heights), shape[axis_at] // parts).reshape((-1,) + (1,) * (len(shape) - 1 - axis_at))
    return loudness


def profile(amount, total, most, lean):
    portions = [(1 << 20) // math.isqrt(rank ** lean) + 1 for rank in range(2, amount + 1)]
    spare, holding = total - most - (amount - 1), [1] * (amount - 1)
    while spare > 0:
        free = [i for i in range(amount - 1) if holding[i] < most]
        whole, budget = sum([portions[i] for i in free]), spare
        for i in free:
            more = min(most - holding[i], max(1, budget * portions[i] // whole), spare)
            holding[i] = holding[i] + more
            spare = spare - more
    return np.array([most] + holding)


def uneven_parts(stream_key, amount, total, most, lean):
    if amount == 2:
        one = jax.random.randint(stream_key, (), max(1, total - most), min(most, total - 1) + 1)
        return jnp.stack([one, total - one])
    sizes = jnp.asarray(profile(amount, total, most, lean), jnp.int32)
    couples = (amount - 1) // 2
    donor, sink = sizes[1:1 + 2 * couples:2], sizes[2:2 + 2 * couples:2]
    slack = jnp.minimum(donor - 1, most - sink)
    shifted = jax.random.randint(jax.random.fold_in(stream_key, 1), (couples,), 0, 1 << 20) % (slack + 1)
    sizes = sizes.at[1:1 + 2 * couples:2].set(donor - shifted).at[2:2 + 2 * couples:2].set(sink + shifted)
    return sizes[jax.random.permutation(jax.random.fold_in(stream_key, 2), amount)]


def centred(key, shape, scale, reach, cuts=(), kind=jnp.bfloat16):
    values = jax.random.normal(key, shape, jnp.float32) * scale
    if len(cuts) > 0:
        values = shard_levels(key, shape, cuts, -0.22, 0.18) * values
    return jnp.clip(values, min=-reach, max=reach).astype(kind)


def setup_inputs(seed: int = 0) -> dict:
    key_list = jax.random.split(jax.random.key(seed), 19)
    return {
        "inputs": draw_inputs(jax.random.fold_in(key_list[18], 71), 0),
        "block_ids": jax.vmap(lambda own: jnp.searchsorted(jnp.cumsum(uneven_parts(own, 2 * LENGTH // BLOCK, LENGTH, BLOCK, 1)), jnp.arange(LENGTH), side="right"))(jax.random.split(key_list[1], SEQS)).reshape((SEQS, LENGTH)).astype(jnp.int32),
        "cotangent": centred(key_list[2], (SEQS, LENGTH, D), 1.0, 6.0, ((0, 4), (1, 8))),
        "ln1_gain": jnp.clip(1.0 + 0.15 * jax.random.normal(key_list[3], (D,), jnp.float32), 0.25, 1.75).astype(jnp.bfloat16),
        "ln1_bias": centred(key_list[4], (D,), 0.3, 1.5, ((0, 32),)),
        "query_weight": centred(key_list[5], (D, D), (D // 4) ** -0.5, 0.25, ((0, 32),)),
        "query_bias": centred(key_list[6], (D,), 0.3, 1.5, ((0, 32),)),
        "key_weight": centred(key_list[7], (D, D), D ** -0.5, 0.125, ((0, 32),)),
        "value_weight": centred(key_list[8], (D, D), D ** -0.5, 0.125, ((0, 32),)),
        "value_bias": centred(key_list[9], (D,), 0.3, 1.5, ((0, 32),)),
        "out_weight": centred(key_list[10], (D, D), (D // 16) ** -0.5, 0.5, ((0, 32),)),
        "out_bias": centred(key_list[11], (D,), 0.3, 1.5, ((0, 32),)),
        "ln2_gain": jnp.clip(1.0 + 0.15 * jax.random.normal(key_list[12], (D,), jnp.float32), 0.25, 1.75).astype(jnp.bfloat16),
        "ln2_bias": centred(key_list[13], (D,), 0.3, 1.5, ((0, 32),)),
        "up_weight": centred(key_list[14], (D, FF), D ** -0.5, 0.125, ((0, 32),)),
        "up_bias": centred(key_list[15], (FF,), 0.3, 1.5, ((0, 32),)),
        "down_weight": centred(key_list[16], (FF, D), (FF // 2) ** -0.5, 0.09375, ((0, 32),)),
        "down_bias": centred(key_list[17], (D,), 0.3, 1.5, ((0, 32),)),
    }


@jax.custom_vjp
def low(v):
    return lax.optimization_barrier(v.astype(jnp.bfloat16)).astype(jnp.float32)

@jax.custom_vjp
def low_back(v):
    return v

def low_keep(v):
    return (low(v), None)

def low_pass(kept, grad):
    return (grad,)

def back_keep(v):
    return (v, None)

def back_low(kept, grad):
    return (low(grad),)
low.defvjp(low_keep, low_pass)
low_back.defvjp(back_keep, back_low)
EPSILON = 1e-05
NEGATIVE = -1e+30
HIGHEST = lax.Precision.HIGHEST

def layer_norm(values, gain, shift):
    center = values - lax.optimization_barrier(jnp.mean(values, axis=-1, keepdims=True))
    spread = lax.optimization_barrier(jnp.mean(center * center, axis=-1, keepdims=True))
    return center * lax.rsqrt(spread + EPSILON) * gain + shift

def matmul(left, right):
    return jnp.dot(left, right, precision=HIGHEST)

def sequence_forward(tokens, params, block_row):
    gain_one, bias_one, query_weight, query_bias, key_weight, value_weight, value_bias, out_weight, out_bias, gain_two, bias_two, up_weight, up_bias, down_weight, down_bias = params
    scale = 1.0 / math.sqrt(HEAD)
    normed = low(layer_norm(tokens, gain_one, bias_one))
    queries = low_back(low((matmul(normed, query_weight) + query_bias) * scale))
    keys = low_back(low(matmul(normed, key_weight)))
    values = low_back(low(matmul(normed, value_weight) + value_bias))
    query_heads = queries.reshape(LENGTH, HEADS, HEAD)
    key_heads = keys.reshape(LENGTH, HEADS, HEAD)
    value_heads = values.reshape(LENGTH, HEADS, HEAD)
    window = min(512, LENGTH)

    def attend(index):
        start = index * window
        query_part = lax.dynamic_slice_in_dim(query_heads, start, window, 0)
        row_ids = lax.dynamic_slice_in_dim(block_row, start, window, 0)
        scores = low_back(jnp.einsum('qhe,khe->hqk', query_part, key_heads, precision=HIGHEST))
        allowed = block_row[None, None, :] <= row_ids[None, :, None]
        scores = jnp.where(allowed, scores, NEGATIVE)
        peak = lax.optimization_barrier(jnp.max(scores, axis=-1, keepdims=True))
        expo = jnp.exp(scores - peak)
        probs = low(expo / lax.optimization_barrier(jnp.sum(expo, axis=-1, keepdims=True)))
        mixed = jnp.einsum('hqk,khe->qhe', probs, value_heads, precision=HIGHEST)
        return mixed.reshape(window, D)
    blocks = lax.map(jax.checkpoint(attend), jnp.arange(LENGTH // window).astype(jnp.int32))
    attended = low_back(low(blocks.reshape(LENGTH, D)))
    branch = low_back(matmul(attended, out_weight) + out_bias)
    hidden_in = tokens + branch
    normed_two = low(layer_norm(hidden_in, gain_two, bias_two))
    pre_act = low_back(matmul(normed_two, up_weight) + up_bias)
    activation = low(jax.nn.gelu(pre_act, approximate=False))
    branch_two = matmul(activation, down_weight) + down_bias
    output = hidden_in + branch_two
    return (output, (jnp.sum(branch * branch), jnp.sum(output * output)))

def reference(inputs, block_ids, cotangent, ln1_gain, ln1_bias, query_weight, query_bias, key_weight, value_weight, value_bias, out_weight, out_bias, ln2_gain, ln2_bias, up_weight, up_bias, down_weight, down_bias):
    params = tuple((weight.astype(jnp.float32) for weight in (ln1_gain, ln1_bias, query_weight, query_bias, key_weight, value_weight, value_bias, out_weight, out_bias, ln2_gain, ln2_bias, up_weight, up_bias, down_weight, down_bias)))
    zeros = tuple((jnp.zeros_like(weight) for weight in params))

    def one_sequence(carry, items):
        totals, branch_sum, mlp_sum = carry
        seq_tokens, block_row, grad_row = items

        def forward(token_values, weights):
            return sequence_forward(token_values, weights, block_row)
        output, pull, squares = jax.vjp(forward, seq_tokens.astype(jnp.float32), params, has_aux=True)
        grad_tokens, grad_weights = pull(grad_row.astype(jnp.float32))
        totals = tuple((total + part for total, part in zip(totals, grad_weights)))
        return ((totals, branch_sum + squares[0], mlp_sum + squares[1]), (output.astype(jnp.bfloat16), grad_tokens))
    start = (zeros, jnp.zeros((), jnp.float32), jnp.zeros((), jnp.float32))
    (totals, branch_sum, mlp_sum), (output, input_grad) = lax.scan(one_sequence, start, (inputs, block_ids, cotangent))
    tokens = inputs.astype(jnp.float32)
    entries = SEQS * LENGTH * D
    rms_input = jnp.sqrt(jnp.sum(tokens * tokens) / entries)
    rms_attention = jnp.sqrt(branch_sum / entries)
    rms_mlp = jnp.sqrt(mlp_sum / entries)
    return (output, input_grad, totals[0], totals[1], totals[2], totals[3], totals[4], totals[5], totals[6], totals[7], totals[8], totals[9], totals[10], totals[11], totals[12], totals[13], totals[14], rms_input, rms_attention, rms_mlp)
```

```python
import math

import jax
import jax.numpy as jnp
from jax import lax
from jax.sharding import PartitionSpec as P

HEAD = 128
EPSILON = 1e-05
NEGATIVE = -1e30
F32 = jnp.float32
BF16 = jnp.bfloat16


def dot(left, right, dims):
    return lax.dot_general(left, right, (dims, ((), ())), preferred_element_type=F32)


def mm(left, right):
    return dot(left, right, ((1,), (0,)))


def mm_lt(left, right):
    return dot(left, right, ((0,), (0,)))


def mm_rt(left, right):
    return dot(left, right, ((1,), (1,)))


def normalize(values):
    center = values - jnp.mean(values, axis=-1, keepdims=True)
    spread = jnp.mean(center * center, axis=-1, keepdims=True)
    inverse = lax.rsqrt(spread + EPSILON)
    return center * inverse, inverse


def normalize_back(normal, inverse, upstream):
    first = jnp.mean(upstream, axis=-1, keepdims=True)
    second = jnp.mean(upstream * normal, axis=-1, keepdims=True)
    return (upstream - first - normal * second) * inverse


def gelu_pair(values):
    half = 0.5 * (1.0 + lax.erf(values * (1.0 / math.sqrt(2.0))))
    density = jnp.exp(-0.5 * values * values) * (1.0 / math.sqrt(2.0 * math.pi))
    return values * half, half + values * density


def core_swap(array):
    size = lax.axis_size("fsdp")
    return lax.ppermute(array, "fsdp", [(f, f ^ 1) for f in range(size)])


def along_chips(array, pairs):
    return lax.ppermute(array, "fsdp", [(2 * a + c, 2 * b + c) for a, b in pairs for c in (0, 1)])


def turned(amount, chips):
    return [(i, (i + amount) % chips) for i in range(chips)]


def roll_first(array, shift):
    size = array.shape[0]
    return lax.dynamic_slice_in_dim(jnp.concatenate([array, array], axis=0), shift, size, 0)


class Line:
    def __init__(self):
        self.size = lax.axis_size("fsdp")
        self.chips = self.size // 2
        self.own = lax.axis_index("fsdp")
        self.chip = self.own // 2
        self.core = self.own % 2
        self.special = self.chips == 4

    def order(self, row):
        if not self.special:
            return row
        parts = row.reshape(self.chips, 2, -1)
        parts = roll_first(parts, self.chip)
        parts = jnp.where(self.core == 0, parts, parts[:, ::-1])
        return parts.transpose(1, 0, 2).reshape(row.shape)

    def gather(self, own):
        if not self.special:
            return lax.all_gather(own, "fsdp", axis=0, tiled=True)
        below = along_chips(own, turned(1, 4))
        above = along_chips(own, turned(3, 4))
        up = along_chips(below, [(1, 2), (2, 3)])
        down = along_chips(above, [(1, 0), (2, 1)])
        far = jnp.where(self.chip >= 2, up, down)
        mine = jnp.concatenate([own, above, far, below], axis=0)
        return jnp.concatenate([mine, core_swap(mine)], axis=0)

    def scatter(self, partial):
        if not self.special:
            whole = partial(slice(None)).astype(BF16)
            return lax.psum_scatter(whole, "fsdp", scatter_dimension=0, tiled=True).astype(F32)
        total = self.size * self.rows
        half = total // 2
        other = partial(slice(half, total)).astype(BF16)
        arrived = core_swap(other)
        mine = partial(slice(0, half)) + arrived.astype(F32)
        rows = self.rows
        own, next_up, far, next_down = (mine[i * rows : (i + 1) * rows] for i in range(4))
        far = far.astype(BF16)
        up = along_chips(far, [(0, 1), (1, 2)])
        down = along_chips(far, [(2, 1), (3, 2)])
        send_up = (next_up + up.astype(F32)).astype(BF16)
        send_down = (next_down + down.astype(F32)).astype(BF16)
        from_below = along_chips(send_up, turned(1, 4))
        from_above = along_chips(send_down, turned(3, 4))
        return own + from_below.astype(F32) + from_above.astype(F32)

    def exchange(self, blocks):
        chips = self.chips
        shape = blocks.shape[1:]
        pairs = roll_first(blocks.reshape((chips, 2) + shape), self.chip)
        arrived = [pairs[0]]
        for step in range(1, chips):
            arrived.append(along_chips(pairs[step], turned(step, chips)))
        stacked = jnp.stack([arrived[0]] + arrived[:0:-1], axis=0)
        keep = lax.dynamic_index_in_dim(stacked, self.core, 1, keepdims=False)
        give = lax.dynamic_index_in_dim(stacked, 1 - self.core, 1, keepdims=False)
        got = core_swap(give)
        both = jnp.where(self.core == 0, jnp.stack([keep, got], 1), jnp.stack([got, keep], 1))
        natural = roll_first(both, (chips - self.chip) % chips)
        return natural.reshape((self.size,) + shape)


def swap_bit(array, axis, bit):
    size = lax.axis_size(axis)
    return lax.ppermute(array, axis, [(i, i ^ bit) for i in range(size)])


def bits(axis):
    size = lax.axis_size(axis)
    return [1 << k for k in range(size.bit_length() - 1)]


def gather_small(own):
    held = own[None]
    for axis in ("fsdp", "dp"):
        index = lax.axis_index(axis)
        for bit in bits(axis):
            got = swap_bit(held, axis, bit)
            high = (index & bit) != 0
            held = jnp.where(
                high, jnp.concatenate([got, held], 0), jnp.concatenate([held, got], 0)
            )
    return held


def sum_small(values):
    for axis in ("dp", "fsdp"):
        for bit in bits(axis):
            values = values + swap_bit(values, axis, bit)
    return values


def local(
    inputs,
    block_ids,
    cotangent,
    ln1_gain,
    ln1_bias,
    query_weight,
    query_bias,
    key_weight,
    value_weight,
    value_bias,
    out_weight,
    out_bias,
    ln2_gain,
    ln2_bias,
    up_weight,
    up_bias,
    down_weight,
    down_bias,
):
    micro, rows, width = inputs.shape
    scale = 1.0 / math.sqrt(HEAD)
    groups = lax.axis_size("dp")
    size = lax.axis_size("fsdp")
    devices = groups * size
    line = Line()
    line.rows = rows
    dp_own = lax.axis_index("dp")
    own = line.own
    slab = width // devices
    span = HEAD // slab
    bands = size // span
    held = groups // span
    band, place = own // span, own % span
    hidden_slab = up_bias.shape[0]
    cols = held * HEAD

    vector = jnp.concatenate(
        [ln1_gain, ln1_bias, query_bias, value_bias, out_bias, ln2_gain, ln2_bias, down_bias, up_bias]
    )
    vectors = gather_small(vector)
    (gain_one, bias_one, query_shift, value_shift, out_shift, gain_two, bias_two, down_shift) = (
        vectors[:, i * slab : (i + 1) * slab].reshape(width).astype(F32) for i in range(8)
    )
    up_shift = vectors[:, 8 * slab :].reshape(groups, size, hidden_slab)
    up_shift = lax.dynamic_index_in_dim(up_shift, own, 1, keepdims=False).reshape(-1).astype(F32)

    def head_columns(row):
        split = row.reshape(span, held, bands, HEAD)
        split = lax.dynamic_index_in_dim(split, place, 0, keepdims=False)
        return lax.dynamic_index_in_dim(split, band, 1, keepdims=False).reshape(cols)

    def head_place(part):
        whole = jnp.zeros((span, held, bands, HEAD), F32)
        part = part.reshape(1, held, 1, HEAD)
        return lax.dynamic_update_slice(whole, part, (place, 0, band, 0)).reshape(width)

    query_shift = head_columns(query_shift)
    value_shift = head_columns(value_shift)

    qkv = jnp.stack([query_weight, key_weight, value_weight], axis=1)
    qkv = qkv.reshape(slab, 3, span, held, bands, HEAD).transpose(4, 2, 0, 1, 3, 5)
    qkv = line.exchange(qkv.reshape(size, slab, 3 * cols))
    qkv_full = lax.all_gather(qkv.reshape(size * slab, 3 * cols), "dp", axis=0, tiled=True)
    tokens_full = [line.gather(inputs[m]) for m in range(micro)]
    out_rows = lax.all_gather(out_weight, "dp", axis=0).reshape(span, held, slab, width)
    out_parts = []
    for step in range(span):
        block = lax.dynamic_index_in_dim(out_rows, place ^ step, 0, keepdims=False)
        out_parts.append(block if step == 0 else swap_bit_any(block, step))
    out_full = unxor(jnp.stack(out_parts, axis=0), place, span)
    out_full = out_full.transpose(1, 0, 2, 3).reshape(cols, width)
    up = up_weight.reshape(slab, groups, size, hidden_slab).transpose(2, 0, 1, 3)
    up = line.exchange(up.reshape(size, slab, groups * hidden_slab))
    up_full = lax.all_gather(up.reshape(size * slab, groups * hidden_slab), "dp", axis=0, tiled=True)
    down_full = lax.all_gather(down_weight, "dp", axis=0, tiled=True)
    grad_full = [line.gather(cotangent[m]) for m in range(micro)]

    input_square = jnp.zeros((), F32)
    branch_square = jnp.zeros((), F32)
    mlp_square = jnp.zeros((), F32)
    normed = []
    heads = []
    probs_all = []
    attended = []
    hidden = []
    for m in range(micro):
        tokens = inputs[m].astype(F32)
        input_square = input_square + jnp.sum(tokens * tokens)
        normal, _ = normalize(tokens_full[m].astype(F32))
        normed_low = (normal * gain_one + bias_one).astype(BF16)
        normed.append(normed_low)
        mixed = mm(normed_low, qkv_full)
        query = ((mixed[:, :cols] + query_shift) * scale).astype(BF16)
        key = mixed[:, cols : 2 * cols].astype(BF16)
        value = (mixed[:, 2 * cols :] + value_shift).astype(BF16)
        ids = line.order(block_ids[m])
        allowed = ids[None, :] <= ids[:, None]
        probs_head = []
        att = []
        for h in range(held):
            cut = slice(h * HEAD, (h + 1) * HEAD)
            scores = jnp.where(allowed, mm_rt(query[:, cut], key[:, cut]), NEGATIVE)
            expo = jnp.exp(scores - jnp.max(scores, axis=-1, keepdims=True))
            probs = expo / jnp.sum(expo, axis=-1, keepdims=True)
            probs_head.append(probs)
            att.append(mm(probs.astype(BF16), value[:, cut]).astype(BF16))
        heads.append((query, key, value))
        probs_all.append(probs_head)
        att = jnp.concatenate(att, axis=1)
        attended.append(att)
        branch = line.scatter(lambda cut: mm(att[cut], out_full)) + out_shift
        branch_square = branch_square + jnp.sum(branch * branch)
        hidden.append(tokens + branch)

    output_rows = []
    normed_two = []
    activation = []
    d_pre_all = []
    d_hidden_all = []
    d_branch_own = []
    gain_two_grad = bias_two_grad = 0.0
    for m in range(micro):
        normal, inverse = normalize(hidden[m])
        normed_two_own = (normal * gain_two + bias_two).astype(BF16)
        n_two = line.gather(normed_two_own)
        normed_two.append(n_two)
        pre = mm(n_two, up_full) + up_shift
        act, slope = gelu_pair(pre)
        act = act.astype(BF16)
        activation.append(act)
        d_pre = (mm_rt(grad_full[m], down_full) * slope).astype(BF16)
        d_pre_all.append(d_pre)
        d_normed_two = line.scatter(lambda cut: mm_rt(d_pre[cut], up_full))
        gain_two_grad = gain_two_grad + jnp.sum(d_normed_two * normal, axis=0)
        bias_two_grad = bias_two_grad + jnp.sum(d_normed_two, axis=0)
        d_hidden = cotangent[m].astype(F32) + normalize_back(normal, inverse, d_normed_two * gain_two)
        d_hidden_all.append(d_hidden)
        d_branch_own.append(d_hidden.astype(BF16))
        branch_two = line.scatter(lambda cut: mm(act[cut], down_full)) + down_shift
        output = hidden[m] + branch_two
        mlp_square = mlp_square + jnp.sum(output * output)
        output_rows.append(output.astype(BF16))

    activation = jnp.concatenate(activation, axis=0)
    grad_cat = jnp.concatenate(grad_full, axis=0)
    d_pre_cat = jnp.concatenate(d_pre_all, axis=0)
    n_two_cat = jnp.concatenate(normed_two, axis=0)
    down_grad = mm_lt(activation, grad_cat).astype(BF16)
    down_sum = lax.psum_scatter(down_grad, "dp", scatter_dimension=0, tiled=True)
    up_grad = mm_lt(n_two_cat, d_pre_cat).astype(BF16)
    up_sum = lax.psum_scatter(up_grad, "dp", scatter_dimension=0, tiled=True)
    up_sum = line.exchange(up_sum.reshape(size, slab, groups * hidden_slab))
    up_sum = up_sum.reshape(size, slab, groups, hidden_slab).transpose(1, 2, 0, 3).reshape(slab, -1)
    up_bias_grad = jnp.sum(d_pre_cat.astype(F32), axis=0)

    d_branch_full = []
    d_heads = []
    d_normed_own = []
    gain_one_grad = bias_one_grad = 0.0
    for m in range(micro):
        d_branch = line.gather(d_branch_own[m])
        d_branch_full.append(d_branch)
        d_att = mm_rt(d_branch, out_full).astype(BF16)
        query, key, value = heads[m]
        d_query, d_key, d_value = [], [], []
        for h in range(held):
            cut = slice(h * HEAD, (h + 1) * HEAD)
            probs = probs_all[m][h]
            d_probs = mm_rt(d_att[:, cut], value[:, cut])
            delta = jnp.sum(probs * d_probs, axis=-1, keepdims=True)
            d_scores = (probs * (d_probs - delta)).astype(BF16)
            d_query.append(mm(d_scores, key[:, cut]).astype(BF16))
            d_key.append(mm_lt(d_scores, query[:, cut]).astype(BF16))
            d_value.append(mm_lt(probs.astype(BF16), d_att[:, cut]).astype(BF16))
        d_qkv = jnp.concatenate(d_query + d_key + d_value, axis=1)
        d_heads.append(d_qkv)

        def terms(cut, d_qkv=d_qkv):
            return mm_rt(d_qkv[cut, :cols], qkv_full[:, :cols]) * scale + mm_rt(
                d_qkv[cut, cols:], qkv_full[:, cols:]
            )

        whole = terms(slice(None))
        normal, _ = normalize(tokens_full[m].astype(F32))
        gain_one_grad = gain_one_grad + jnp.sum(whole * normal, axis=0)
        bias_one_grad = bias_one_grad + jnp.sum(whole, axis=0)
        d_normed_own.append(line.scatter(lambda cut: whole[cut]))

    d_heads = jnp.concatenate(d_heads, axis=0)
    d_branch_full = jnp.concatenate(d_branch_full, axis=0)
    attended = jnp.concatenate(attended, axis=0)
    normed = jnp.concatenate(normed, axis=0)
    qkv_grad = mm_lt(normed, d_heads)
    qkv_grad = jnp.concatenate([qkv_grad[:, :cols] * scale, qkv_grad[:, cols:]], axis=1).astype(BF16)
    out_grad = mm_lt(attended, d_branch_full).astype(BF16)
    out_grad = out_grad.reshape(held, span, slab, width).transpose(1, 0, 2, 3)
    out_parts = []
    for step in range(span):
        block = lax.dynamic_index_in_dim(out_grad, place ^ step, 0, keepdims=False)
        out_parts.append(block if step == 0 else swap_bit_any(block, step))
    out_grad = unxor(jnp.stack(out_parts, axis=0), place, span).reshape(groups * slab, width)
    out_sum = lax.psum_scatter(out_grad, "dp", scatter_dimension=0, tiled=True)
    qkv_sum = lax.psum_scatter(qkv_grad, "dp", scatter_dimension=0, tiled=True)
    qkv_sum = line.exchange(qkv_sum.reshape(size, slab, 3 * cols))
    qkv_sum = qkv_sum.reshape(bands, span, slab, 3, held, HEAD).transpose(3, 2, 1, 4, 0, 5)
    qkv_sum = qkv_sum.reshape(3, slab, width).astype(F32)

    d_heads_sum = jnp.sum(d_heads.astype(F32), axis=0)
    out_bias_grad = sum(jnp.sum(part.astype(F32), axis=0) for part in d_branch_own)
    down_bias_grad = sum(jnp.sum(cotangent[m].astype(F32), axis=0) for m in range(micro))

    input_rows = []
    for m in range(micro):
        normal, inverse = normalize(inputs[m].astype(F32))
        input_rows.append(
            d_hidden_all[m] + normalize_back(normal, inverse, d_normed_own[m] * gain_one)
        )

    up_bias_whole = jnp.zeros((groups, size, hidden_slab), F32)
    up_bias_whole = lax.dynamic_update_slice(
        up_bias_whole, up_bias_grad.reshape(groups, 1, hidden_slab), (0, own, 0)
    ).reshape(-1)
    scalars = jnp.stack([input_square, branch_square, mlp_square])
    scalars = jnp.concatenate([scalars, jnp.zeros((HEAD - 3,), F32)])
    early = sum_small(
        jnp.concatenate(
            [scalars, down_bias_grad, gain_two_grad, bias_two_grad, out_bias_grad, up_bias_whole]
        )
    )
    late = sum_small(
        jnp.concatenate(
            [
                gain_one_grad,
                bias_one_grad,
                head_place(d_heads_sum[:cols] * scale),
                head_place(d_heads_sum[2 * cols :]),
            ]
        )
    )
    index = dp_own * size + own

    def own_part(whole, start, length):
        return lax.dynamic_slice_in_dim(whole, start + index * length, length, 0)

    rms = jnp.sqrt(early[:3] / (micro * rows * devices * width))
    down_bias_sum, gain_two_sum, bias_two_sum, out_bias_sum = (
        own_part(early, HEAD + i * width, slab) for i in range(4)
    )
    up_bias_sum = own_part(early, HEAD + 4 * width, hidden_slab)
    gain_one_sum, bias_one_sum, query_bias_sum, value_bias_sum = (
        own_part(late, i * width, slab) for i in range(4)
    )
    return (
        jnp.stack(output_rows, axis=0),
        jnp.stack(input_rows, axis=0),
        gain_one_sum,
        bias_one_sum,
        qkv_sum[0],
        query_bias_sum,
        qkv_sum[1],
        qkv_sum[2],
        value_bias_sum,
        out_sum.astype(F32),
        out_bias_sum,
        gain_two_sum,
        bias_two_sum,
        up_sum.astype(F32),
        up_bias_sum,
        down_sum.astype(F32),
        down_bias_sum,
        rms[0],
        rms[1],
        rms[2],
    )


def swap_bit_any(array, step):
    size = lax.axis_size("fsdp")
    return lax.ppermute(array, "fsdp", [(i, i ^ step) for i in range(size)])


def unxor(parts, place, span):
    bit = 1
    while bit < span:
        shape = parts.shape
        split = parts.reshape((span // (2 * bit), 2, bit) + shape[1:])
        split = jnp.where((place & bit) != 0, split[:, ::-1], split)
        parts = split.reshape(shape)
        bit *= 2
    return parts


def solution(mesh):
    shard = P(("dp", "fsdp"))
    matrix = P(("dp", "fsdp"), None)
    rows = P("dp", "fsdp", None)
    in_specs = (
        rows,
        P("dp", None),
        rows,
        shard,
        shard,
        matrix,
        shard,
        matrix,
        matrix,
        shard,
        matrix,
        shard,
        shard,
        shard,
        matrix,
        shard,
        matrix,
        shard,
    )
    out_specs = (
        rows,
        rows,
        shard,
        shard,
        matrix,
        shard,
        matrix,
        matrix,
        shard,
        matrix,
        shard,
        shard,
        shard,
        matrix,
        shard,
        matrix,
        shard,
        P(),
        P(),
        P(),
    )
    return jax.shard_map(local, mesh=mesh, in_specs=in_specs, out_specs=out_specs, check_vma=False)
```
